32 devices in a mesh: grp: 4 (over x, core), vocab: 8 (over z, y).
Axes of the slice: x: 2, y: 2, z: 4, core: 2. Of those that a mesh axis runs over, the one named last changes fastest.
Arguments:
- hidden: bfloat16 [256, 4096], P(('grp', 'vocab')), parts along dimension 0
- head: bfloat16 [4096, 24576], P(None, 'vocab'), may hold values from -0.09375 to 0.09375
- block_ids: int32 [256, 16], P('grp'), parts along dimension 0, may hold values from 0 to 191, as said below
- valid_count: int32 [256], P('grp'), parts along dimension 0, may hold values from 1 to 16, as said below
- beam_order: int32 [256], P('grp'), parts along dimension 0, may hold values from 0 to 63, each once
Outputs:
- block_logprobs: float32 [256, 16, 128], P(('grp', 'vocab')), parts along dimension 0
The draws below stay inside these ranges and needn't reach their ends.
There are 4 independent parts, one for each index of `grp`. The reference program is written for one: setup_inputs(seed, part) draws one part's arguments, and reference() takes and returns one part's arrays. A program takes and returns all parts, laid end to end along the dimension named above; an argument that names none is the same for every part. Nothing has to cross between parts.
Inputs may be any that keep to these rules, and one draw needn't show every extreme that they name: `block_ids`: vocabulary block b holds entries 128 * b to 128 * b + 127 and lies on vocabulary device b // 24. Among the 128 slots of the output rows of one vocabulary device, at most 16 name blocks of any one vocabulary device, and exactly 16 do for one of them. `valid_count`: some output row has all 16 slots valid.
All inputs are finite; a program needn't handle non-finite values.
Results may differ from the reference program's by a relative error of at most 0.0003.
Values may be sent and summed in bfloat16 or wider, within the bound.
No kernel may reach another device: no remote copies, remote signals or barrier semaphores. Data moves between devices by JAX's collectives and lax.ppermute only.
A program may use at most 128 MiB of HBM per device.

```python
import jax
import jax.numpy as jnp

D = 4096
B_DEV = 8
K = 16
BLK = 128
BLOCKS_DEV = 24
CAP = 16
BEAMS = 64
V = 24576
NB = 192
N_VOCAB = 8


def draw_hidden(key, part):
    key = jax.random.fold_in(key, 5)
    key_base = jax.random.fold_in(key, 0)
    base = jnp.clip(jax.random.normal(key_base, (BEAMS, D), jnp.float32), -6.0, 6.0)
    return (3.0 * base).astype(jnp.bfloat16)


def draw_block_ids(key, part):
    key = jax.random.fold_in(key, 11)
    key_hot, key_order, key_local = jax.random.split(key, 3)
    entries = B_DEV * K
    hot = jax.random.randint(key_hot, (N_VOCAB, 1), 0, N_VOCAB)
    order = jax.vmap(lambda sub: jax.random.permutation(sub, entries))(jax.random.split(key_order, N_VOCAB))
    offset = jnp.where(order < CAP, 0, 1 + (order - CAP) % (N_VOCAB - 1))
    device = (hot + offset) % N_VOCAB
    local = jax.random.randint(key_local, (N_VOCAB, entries), 0, BLOCKS_DEV)
    return (device * BLOCKS_DEV + local).reshape(BEAMS, K).astype(jnp.int32)


def draw_valid_count(key, part):
    key = jax.random.fold_in(key, 17)
    key_count, key_full = jax.random.split(key)
    counts = jax.random.randint(key_count, (BEAMS,), 1, K + 1)
    full = jax.random.randint(key_full, (), 0, BEAMS)
    return jnp.where(jnp.arange(BEAMS) == full, K, counts).astype(jnp.int32)


def block_scale(own_key, extent, pieces, least, high):
    def one(axis_at, parts):
        heights = jax.random.uniform(jax.random.fold_in(jax.random.fold_in(own_key, 6), axis_at), (parts,), jnp.float32, least / len(pieces), high / len(pieces))
        return jnp.repeat(jnp.exp(heights), extent[axis_at] // parts).reshape((-1,) + (1,) * (len(extent) - axis_at - 1))

    level = one(*pieces[0])
    for cut in pieces[1:]:
        level = level * one(*cut)
    return level


def centred(stream_key, shape, deviation, most, pieces=(), kind=jnp.bfloat16):
    loudness = block_scale(stream_key, shape, pieces, -0.22, 0.18) if pieces else 1.0
    result = jax.random.normal(stream_key, shape, jnp.float32) * deviation * loudness
    return jnp.minimum(jnp.maximum(result, -most), most).astype(kind)


def setup_inputs(seed: int = 0, part: int = 0) -> dict:
    seeds = jax.random.split(jax.random.key(seed), 6)
    part_keys = jax.random.split(jax.random.fold_in(seeds[5], part), 6)
    hidden = draw_hidden(jax.random.fold_in(jax.random.fold_in(seeds[5], part), 71), part)
    head = centred(seeds[1], (D, V), D ** -0.5, 0.09375, ((1, 8),))
    block_ids = draw_block_ids(jax.random.fold_in(jax.random.fold_in(seeds[5], part), 71), part)
    valid_count = draw_valid_count(jax.random.fold_in(jax.random.fold_in(seeds[5], part), 71), part)
    beam_order = jax.random.permutation(part_keys[4], BEAMS).astype(jnp.int32)
    return dict(hidden=hidden, head=head, block_ids=block_ids, valid_count=valid_count, beam_order=beam_order)


def reference(hidden, head, block_ids, valid_count, beam_order):
    logits = jnp.dot(hidden, head, preferred_element_type=jnp.float32)
    top = jnp.max(logits, axis=1)
    lse = top + jnp.log(jnp.sum(jnp.exp(logits - top[:, None]), axis=1))
    rows = logits[beam_order]
    blocks = rows.reshape(BEAMS, NB, BLK)
    row_index = jnp.arange(BEAMS, dtype=jnp.int32)[:, None]
    tiles = blocks[row_index, block_ids]
    tiles = tiles - lse[beam_order][:, None, None]
    valid = jnp.arange(K, dtype=jnp.int32)[None, :] < valid_count[:, None]
    return jnp.where(valid[:, :, None], tiles, jnp.float32(0.0))
```

```python
import functools

import jax
import jax.numpy as jnp
from jax import lax
from jax.experimental import pallas as pl
from jax.experimental.pallas import tpu as pltpu
from jax.sharding import PartitionSpec as P

BLK = 128
CAP = 16
NEAR = 4


def exchange(x, n, mask):
    return lax.ppermute(x, "vocab", [(i, i ^ mask) for i in range(n)])


def score_kernel(n, rows_dev, me_ref, src_ref, order_ref, near_ref, far_ref, head_ref, *refs):
    outs, (x, logits, stats) = refs[:NEAR], refs[NEAR:]
    half = near_ref.shape[0]
    beams = 2 * half
    blocks = head_ref.shape[1] // BLK
    group = 8 if blocks % 8 == 0 else 1
    x[:half, :] = near_ref[...]
    x[half:, :] = far_ref[...]
    for j in range(0, blocks, group):
        product = jnp.dot(x[...], head_ref[:, j * BLK : (j + group) * BLK], preferred_element_type=jnp.float32)
        for i in range(group):
            logits[(j + i) * beams : (j + i + 1) * beams, :] = product[:, i * BLK : (i + 1) * BLK]
    most = functools.reduce(jnp.maximum, [logits[j * beams : (j + 1) * beams, :] for j in range(blocks)])
    most = jnp.max(most, axis=1, keepdims=True)
    total = sum(jnp.exp(logits[j * beams : (j + 1) * beams, :] - most) for j in range(blocks))
    lse = most + jnp.log(jnp.sum(total, axis=1, keepdims=True))
    stats[...] = jnp.broadcast_to(lse, (beams, BLK))
    me = me_ref[0]
    for near in range(NEAR):
        for far in range(n // NEAR):
            owner = me ^ (far * NEAR + near)
            for k in range(CAP):
                outs[near][far, k : k + 1, :] = logits[pl.ds(src_ref[owner * CAP + k], 1), :]
            for i in range(rows_dev):
                outs[near][far, CAP + i : CAP + i + 1, :] = stats[pl.ds(order_ref[owner * rows_dev + i], 1), :]


def place_kernel(n, rows_dev, slots, at_ref, *refs):
    own, others, out_ref, held = refs[:NEAR], refs[NEAR : NEAR + n // NEAR - 1], refs[-2], refs[-1]
    size = CAP + rows_dev
    for near in range(NEAR):
        held[near * size : (near + 1) * size, :] = own[near][0]
        for far in range(1, n // NEAR):
            base = (far * NEAR + near) * size
            held[base : base + size, :] = others[far - 1][near]
    parts = [held[d * size + CAP : (d + 1) * size, :] for d in range(n)]
    most = functools.reduce(jnp.maximum, parts)
    lse = most + jnp.log(sum(jnp.exp(part - most) for part in parts))
    for r in range(rows_dev):
        for k in range(slots):
            at = at_ref[r * slots + k]
            tile = held[pl.ds(jnp.maximum(at, 0), 1), :] - lse[r : r + 1, :]
            out_ref[r, k : k + 1, :] = jnp.where(at >= 0, tile, jnp.float32(0.0))


def body(n, hidden, head, block_ids, valid_count, beam_order):
    me = lax.axis_index("vocab").astype(jnp.int32)
    rows_dev = hidden.shape[0]
    slots = block_ids.shape[1]
    blocks_dev = head.shape[1] // BLK
    per_owner = rows_dev * slots
    size = CAP + rows_dev
    vmem = pl.BlockSpec(memory_space=pltpu.VMEM)
    smem = pl.BlockSpec(memory_space=pltpu.SMEM)

    apart = (beam_order // rows_dev) ^ me
    row_of = ((apart & 1) * (n // 2) + (apart >> 1)) * rows_dev + beam_order % rows_dev

    ids = block_ids.reshape(n, per_owner)
    device = ids // blocks_dev
    local = ids % blocks_dev
    before = jnp.arange(per_owner)[:, None] > jnp.arange(per_owner)[None, :]
    mine = device == me
    rank = jnp.sum(jnp.where(mine[:, None, :] & before[None], 1, 0), axis=2)
    code = jnp.repeat(row_of.reshape(n, rows_dev), slots, axis=1) + local * (n * rows_dev)
    chosen = mine[:, None, :] & (rank[:, None, :] == jnp.arange(CAP)[None, :, None])
    src = jnp.sum(jnp.where(chosen, code[:, None, :], 0), axis=2).reshape(-1)

    my_ids = lax.dynamic_slice_in_dim(device, me, 1, axis=0)[0]
    my_count = lax.dynamic_slice_in_dim(valid_count, me * rows_dev, rows_dev)
    my_rank = jnp.sum(jnp.where((my_ids[:, None] == my_ids[None, :]) & before, 1, 0), axis=1)
    valid = (jnp.arange(slots)[None, :] < my_count[:, None]).reshape(-1)
    at = jnp.where(valid, (my_ids ^ me) * size + my_rank, -1)

    near = jnp.concatenate([hidden] + [exchange(hidden, n, 2 * t) for t in range(1, n // 2)], axis=0)
    far = exchange(near, n, 1)

    shape = jax.ShapeDtypeStruct((n // NEAR, size, BLK), jnp.float32)
    beams = n * rows_dev
    sent = pl.pallas_call(
        functools.partial(score_kernel, n, rows_dev),
        out_shape=[shape] * NEAR,
        in_specs=[smem, smem, smem, vmem, vmem, vmem],
        out_specs=[vmem] * NEAR,
        scratch_shapes=[pltpu.VMEM((beams, hidden.shape[1]), hidden.dtype), pltpu.VMEM((blocks_dev * beams, BLK), jnp.float32), pltpu.VMEM((beams, BLK), jnp.float32)],
        compiler_params=pltpu.CompilerParams(vmem_limit_bytes=24 * 2**20),
        name="score",
    )(me.reshape(1), src, row_of, near, far, pltpu.with_memory_space_constraint(head, pltpu.VMEM))

    own = [sent[0]] + [exchange(sent[i], n, i) for i in range(1, NEAR)]
    others = [
        exchange(jnp.stack([part[j] for part in own]), n, NEAR * j) for j in range(1, n // NEAR)
    ]
    return pl.pallas_call(
        functools.partial(place_kernel, n, rows_dev, slots),
        out_shape=jax.ShapeDtypeStruct((rows_dev, slots, BLK), jnp.float32),
        in_specs=[smem] + [vmem] * (NEAR + n // NEAR - 1),
        out_specs=vmem,
        scratch_shapes=[pltpu.VMEM((n * size, BLK), jnp.float32)],
        name="place",
    )(at, *own, *others)


def solution(mesh):
    return jax.shard_map(
        functools.partial(body, mesh.shape["vocab"]),
        mesh=mesh,
        in_specs=(P(("grp", "vocab"), None), P(None, "vocab"), P("grp", None), P("grp"), P("grp")),
        out_specs=P(("grp", "vocab"), None, None),
        check_vma=False,
    )
```

```python
import functools

import jax
import jax.numpy as jnp
from jax import lax
from jax.experimental import pallas as pl
from jax.experimental.pallas import tpu as pltpu
from jax.sharding import PartitionSpec as P

BLK = 128
CAP = 16
NEAR = 4


def exchange(x, n, mask):
    return lax.ppermute(x, "vocab", [(i, i ^ mask) for i in range(n)])


def split(n, rows_dev):
    beams = n * rows_dev
    at = lax.broadcasted_iota(jnp.int32, (beams, beams), 0)
    to = lax.broadcasted_iota(jnp.int32, (beams, beams), 1)
    shift = rows_dev.bit_length() - 1
    same = (at >> shift) == (to >> shift)
    return same.astype(jnp.bfloat16), (same & (at < to)).astype(jnp.bfloat16)


def counts(a, b):
    return jnp.dot(a, b, preferred_element_type=jnp.float32)


def fetch_kernel(
    n,
    rows_dev,
    blocks_dev,
    me_ref,
    ids_hbm,
    valid_hbm,
    order_hbm,
    head_hbm,
    after,
    src_ref,
    rows_ref,
    at_ref,
    held_ref,
    ids_ref,
    valid_ref,
    order_ref,
    sems,
):
    copies = [
        pltpu.make_async_copy(ids_hbm, ids_ref, sems.at[0]),
        pltpu.make_async_copy(valid_hbm, valid_ref, sems.at[1]),
        pltpu.make_async_copy(order_hbm, order_ref, sems.at[2]),
        pltpu.make_async_copy(head_hbm.at[:, : held_ref.shape[1]], held_ref, sems.at[3]),
    ]
    for copy in copies:
        copy.start()
    for copy in copies[:3]:
        copy.wait()
    me = me_ref[0]
    slots, beams = ids_ref.shape
    shift = rows_dev.bit_length() - 1
    apart = (order_ref[...] >> shift) ^ me
    row_of = ((apart & (NEAR - 1)) * (n // NEAR) + (apart >> (NEAR.bit_length() - 1))) * rows_dev
    row_of = row_of + (order_ref[...] & (rows_dev - 1))
    rows_ref[...] = row_of

    ids = ids_ref[...]
    same, earlier = split(n, rows_dev)
    k_at = lax.broadcasted_iota(jnp.int32, (slots, slots), 0)
    k_to = lax.broadcasted_iota(jnp.int32, (slots, slots), 1)
    below = (k_to < k_at).astype(jnp.bfloat16)

    def rank(on):
        ones = jnp.where(on, 1.0, 0.0).astype(jnp.bfloat16)
        return (counts(ones, earlier) + counts(below, counts(ones, same).astype(jnp.bfloat16))).astype(jnp.int32)

    at = jnp.zeros((slots, beams), jnp.int32)
    for d in range(n):
        on = (ids >= d * blocks_dev) & (ids < (d + 1) * blocks_dev)
        at = jnp.where(on, (me ^ d) * (CAP + rows_dev) + rank(on), at)
    k_index = lax.broadcasted_iota(jnp.int32, (slots, beams), 0)
    at_ref[...] = jnp.where(k_index < valid_ref[...], at, -1)

    first = me * blocks_dev
    mine = (ids >= first) & (ids < first + blocks_dev)
    my_rank = jnp.where(mine, rank(mine), -1)
    local = ids - first
    owner = (
        (lax.broadcasted_iota(jnp.int32, (beams, n), 0) >> shift) == lax.broadcasted_iota(jnp.int32, (beams, n), 1)
    ).astype(jnp.bfloat16)
    rows = jnp.broadcast_to(row_of, (slots, beams))

    def gathered(value):
        picked = [jnp.sum(jnp.where(my_rank == j, value, 0), axis=0, keepdims=True) for j in range(CAP)]
        table = jnp.concatenate(picked, axis=0).astype(jnp.float32).astype(jnp.bfloat16)
        return counts(table, owner).astype(jnp.int32)

    src_ref[...] = gathered(local) * beams + gathered(rows)
    copies[3].wait()


def score_kernel(n, rows_dev, me_ref, src_vmem, rows_vmem, x_ref, held_ref, head_hbm, *refs):
    outs, (rest, logits, stats, src_ref, rows_ref, sems, index_sems) = refs[:NEAR], refs[NEAR:]
    beams = x_ref.shape[0]
    held = held_ref.shape[1]
    blocks = head_hbm.shape[1] // BLK
    step = rest.shape[2]
    chunks = [
        pltpu.make_async_copy(head_hbm.at[:, held + c * step : held + (c + 1) * step], rest.at[c], sems.at[c])
        for c in range(rest.shape[0])
    ]
    copies = [
        pltpu.make_async_copy(src_vmem, src_ref, index_sems.at[0]),
        pltpu.make_async_copy(rows_vmem, rows_ref, index_sems.at[1]),
    ]
    for copy in chunks + copies:
        copy.start()

    def multiply(columns, base):
        product = jnp.dot(x_ref[...], columns, preferred_element_type=jnp.float32)
        for i in range(step // BLK):
            logits[(base + i) * beams : (base + i + 1) * beams, :] = product[:, i * BLK : (i + 1) * BLK]

    for c in range(held // step):
        multiply(held_ref[:, c * step : (c + 1) * step], c * (step // BLK))
    for c, chunk in enumerate(chunks):
        chunk.wait()
        multiply(rest[c], (held + c * step) // BLK)
    most = functools.reduce(jnp.maximum, [logits[j * beams : (j + 1) * beams, :] for j in range(blocks)])
    most = jnp.max(most, axis=1, keepdims=True)
    total = sum(jnp.exp(logits[j * beams : (j + 1) * beams, :] - most) for j in range(blocks))
    lse = most + jnp.log(jnp.sum(total, axis=1, keepdims=True))
    stats[...] = jnp.broadcast_to(lse, (beams, BLK))
    for copy in copies:
        copy.wait()
    me = me_ref[0]
    for near in range(NEAR):
        for far in range(n // NEAR):
            owner = me ^ (far * NEAR + near)
            for k in range(CAP):
                outs[near][far, k : k + 1, :] = logits[pl.ds(src_ref[k, owner], 1), :]
            for i in range(rows_dev):
                outs[near][far, CAP + i : CAP + i + 1, :] = stats[pl.ds(rows_ref[0, owner * rows_dev + i], 1), :]


def place_kernel(n, rows_dev, slots, me_ref, at_vmem, *refs):
    own, others = refs[:NEAR], refs[NEAR : NEAR + n // NEAR - 1]
    out_ref, held, at_ref, sem = refs[-4:]
    copy = pltpu.make_async_copy(at_vmem, at_ref, sem)
    copy.start()
    size = CAP + rows_dev
    for near in range(NEAR):
        held[near * size : (near + 1) * size, :] = own[near][0]
        for far in range(1, n // NEAR):
            base = (far * NEAR + near) * size
            held[base : base + size, :] = others[far - 1][near]
    parts = [held[d * size + CAP : (d + 1) * size, :] for d in range(n)]
    most = functools.reduce(jnp.maximum, parts)
    lse = most + jnp.log(sum(jnp.exp(part - most) for part in parts))
    copy.wait()
    first = me_ref[0] * rows_dev
    for r in range(rows_dev):
        for k in range(slots):
            at = at_ref[k, first + r]
            tile = held[pl.ds(jnp.maximum(at, 0), 1), :] - lse[r : r + 1, :]
            out_ref[r, k : k + 1, :] = jnp.where(at >= 0, tile, jnp.float32(0.0))


def in_vmem(x):
    return pltpu.with_memory_space_constraint(x, pltpu.VMEM)


def in_hbm(x):
    return pltpu.with_memory_space_constraint(x, pltpu.HBM)


def body(n, hidden, head, block_ids, valid_count, beam_order):
    me = lax.axis_index("vocab").astype(jnp.int32).reshape(1)
    rows_dev = hidden.shape[0]
    beams, slots = block_ids.shape
    blocks_dev = head.shape[1] // BLK
    size = CAP + rows_dev
    fars = n // NEAR
    depth = head.shape[0]
    held = blocks_dev // 2 * BLK
    step = 4 * BLK if held % (4 * BLK) == 0 and (head.shape[1] - held) % (4 * BLK) == 0 else BLK
    vmem = pl.BlockSpec(memory_space=pltpu.VMEM)
    smem = pl.BlockSpec(memory_space=pltpu.SMEM)
    hbm = pl.BlockSpec(memory_space=pltpu.HBM)
    anywhere = pl.BlockSpec(memory_space=pl.ANY)

    far = [exchange(hidden, n, NEAR * f) for f in range(1, fars)]
    near = [exchange(hidden, n, i) for i in range(1, NEAR)]
    far = far[0] if fars == 2 else jnp.concatenate(far, axis=0)
    src, row_of, at, first = pl.pallas_call(
        functools.partial(fetch_kernel, n, rows_dev, blocks_dev),
        out_shape=[
            jax.ShapeDtypeStruct((CAP, n), jnp.int32),
            jax.ShapeDtypeStruct((1, beams), jnp.int32),
            jax.ShapeDtypeStruct((slots, beams), jnp.int32),
            pltpu.VMEM((depth, held), head.dtype),
        ],
        in_specs=[smem, hbm, hbm, hbm, hbm, anywhere],
        out_specs=[vmem] * 4,
        scratch_shapes=[
            pltpu.VMEM((slots, beams), jnp.int32),
            pltpu.VMEM((1, beams), jnp.int32),
            pltpu.VMEM((1, beams), jnp.int32),
            pltpu.SemaphoreType.DMA((4,)),
        ],
        cost_estimate=pl.CostEstimate(flops=0, bytes_accessed=2 * depth * held, transcendentals=0),
        compiler_params=pltpu.CompilerParams(vmem_limit_bytes=4 * 2**20),
        name="fetch",
    )(
        me,
        in_hbm(block_ids.T),
        in_hbm(valid_count.reshape(1, beams)),
        in_hbm(beam_order.reshape(1, beams)),
        in_hbm(head),
        far,
    )

    passed = [exchange(far, n, i) for i in range(1, NEAR)]
    x = jnp.concatenate([hidden, far] + [part for pair in zip(near, passed) for part in pair], axis=0)

    shape = jax.ShapeDtypeStruct((fars, size, BLK), jnp.float32)
    sent = pl.pallas_call(
        functools.partial(score_kernel, n, rows_dev),
        out_shape=[shape] * NEAR,
        in_specs=[smem, vmem, vmem, vmem, vmem, hbm],
        out_specs=[vmem] * NEAR,
        scratch_shapes=[
            pltpu.VMEM(((head.shape[1] - held) // step, depth, step), head.dtype),
            pltpu.VMEM((blocks_dev * beams, BLK), jnp.float32),
            pltpu.VMEM((beams, BLK), jnp.float32),
            pltpu.SMEM((CAP, n), jnp.int32),
            pltpu.SMEM((1, beams), jnp.int32),
            pltpu.SemaphoreType.DMA(((head.shape[1] - held) // step,)),
            pltpu.SemaphoreType.DMA((2,)),
        ],
        compiler_params=pltpu.CompilerParams(vmem_limit_bytes=24 * 2**20),
        name="score",
    )(me, in_vmem(src), in_vmem(row_of), in_vmem(x), in_vmem(first), in_hbm(head))

    own = [sent[0]] + [exchange(sent[i], n, i) for i in range(1, NEAR)]
    others = [exchange(jnp.stack([part[j] for part in own]), n, NEAR * j) for j in range(1, fars)]
    return pl.pallas_call(
        functools.partial(place_kernel, n, rows_dev, slots),
        out_shape=jax.ShapeDtypeStruct((rows_dev, slots, BLK), jnp.float32),
        in_specs=[smem, vmem] + [vmem] * (NEAR + fars - 1),
        out_specs=vmem,
        scratch_shapes=[
            pltpu.VMEM((n * size, BLK), jnp.float32),
            pltpu.SMEM((slots, beams), jnp.int32),
            pltpu.SemaphoreType.DMA,
        ],
        name="place",
    )(me, in_vmem(at), *map(in_vmem, own), *map(in_vmem, others))


def solution(mesh):
    return jax.shard_map(
        functools.partial(body, mesh.shape["vocab"]),
        mesh=mesh,
        in_specs=(P(("grp", "vocab"), None), P(None, "vocab"), P("grp", None), P("grp"), P("grp")),
        out_specs=P(("grp", "vocab"), None, None),
        check_vma=False,
    )
```

```python
import functools

import jax
import jax.numpy as jnp
from jax import lax
from jax.experimental import pallas as pl
from jax.experimental.pallas import tpu as pltpu
from jax.sharding import PartitionSpec as P

BLK = 128
CAP = 16
NEAR = 4
ORDER = (0, 3, 1, 2)
FIRST = (0, 4)
SECOND = (0, 3, 1, 2)
PAD = 8


def exchange(x, n, mask):
    return lax.ppermute(x, "vocab", [(i, i ^ mask) for i in range(n)])


def split(n, rows_dev):
    beams = n * rows_dev
    at = lax.broadcasted_iota(jnp.int32, (beams, beams), 0)
    to = lax.broadcasted_iota(jnp.int32, (beams, beams), 1)
    shift = rows_dev.bit_length() - 1
    same = (at >> shift) == (to >> shift)
    return same.astype(jnp.bfloat16), (same & (at < to)).astype(jnp.bfloat16)


def mark_kernel(me_ref, out_ref):
    out_ref[...] = jnp.full(out_ref.shape, me_ref[0], jnp.int32)


def counts(a, b):
    return jnp.dot(a, b, preferred_element_type=jnp.float32)


def index_kernel(
    n,
    rows_dev,
    blocks_dev,
    me_ref,
    ids_hbm,
    valid_hbm,
    order_hbm,
    mark,
    after,
    hidden_hbm,
    src_ref,
    rows_ref,
    place_ref,
    own_ref,
    ids_ref,
    valid_ref,
    order_ref,
    sems,
):
    copies = [
        pltpu.make_async_copy(ids_hbm, ids_ref, sems.at[0]),
        pltpu.make_async_copy(valid_hbm, valid_ref, sems.at[1]),
        pltpu.make_async_copy(order_hbm, order_ref, sems.at[2]),
    ]
    own = pltpu.make_async_copy(hidden_hbm, own_ref, sems.at[3])
    for copy in copies + [own]:
        copy.start()
    for copy in copies:
        copy.wait()
    me = me_ref[0]
    slots, beams = ids_ref.shape
    shift = rows_dev.bit_length() - 1
    apart = (order_ref[...] >> shift) ^ me
    near = apart & (NEAR - 1)
    place = sum(jnp.where(near == mask, i, 0) for i, mask in enumerate(ORDER))
    row_of = ((place * (n // NEAR) + (apart >> (NEAR.bit_length() - 1)) + n - 1) & (n - 1)) * rows_dev
    row_of = row_of + (order_ref[...] & (rows_dev - 1))
    rows_ref[...] = jnp.full(rows_ref.shape, -1, jnp.int32)
    rows_ref[:, : order_ref.shape[1]] = row_of

    ids = ids_ref[...]
    same, earlier = split(n, rows_dev)
    k_at = lax.broadcasted_iota(jnp.int32, (slots, slots), 0)
    k_to = lax.broadcasted_iota(jnp.int32, (slots, slots), 1)
    below = (k_to < k_at).astype(jnp.bfloat16)

    def rank(on):
        ones = jnp.where(on, 1.0, 0.0).astype(jnp.bfloat16)
        return (counts(ones, earlier) + counts(below, counts(ones, same).astype(jnp.bfloat16))).astype(jnp.int32)

    at = jnp.zeros((slots, beams), jnp.int32)
    for d in range(n):
        on = (ids >= d * blocks_dev) & (ids < (d + 1) * blocks_dev)
        at = jnp.where(on, (me ^ d) * CAP + rank(on), at)
    k_index = lax.broadcasted_iota(jnp.int32, (slots, beams), 0)
    at = jnp.where(k_index < valid_ref[...], at, -1)
    row_index = lax.broadcasted_iota(jnp.int32, (slots, beams), 1)
    total = place_ref.shape[1]
    for r in range(rows_dev):
        column = jnp.sum(jnp.where(row_index == me * rows_dev + r, at, 0), axis=1, keepdims=True)
        hit = lax.broadcasted_iota(jnp.int32, (slots, total), 1) == column
        place_ref[r * slots : (r + 1) * slots, :] = jnp.where(hit, 1.0, 0.0)
    first = me * blocks_dev
    mine = (ids >= first) & (ids < first + blocks_dev)
    my_rank = jnp.where(mine, rank(mine), -1)
    local = ids - first
    owner = (
        (lax.broadcasted_iota(jnp.int32, (beams, n), 0) >> shift) == lax.broadcasted_iota(jnp.int32, (beams, n), 1)
    ).astype(jnp.bfloat16)
    rows = jnp.broadcast_to(row_of, (slots, beams))

    def gathered(value):
        picked = [jnp.sum(jnp.where(my_rank == j, value, 0), axis=0, keepdims=True) for j in range(CAP)]
        table = jnp.concatenate(picked, axis=0).astype(jnp.float32).astype(jnp.bfloat16)
        return counts(table, owner).astype(jnp.int32)

    src_ref[...] = gathered(local) * beams + gathered(rows)
    own.wait()


def second_masks(n):
    used = functools.reduce(lambda a, b: a | b, FIRST)
    masks = [mask for mask in range(n) if mask & used == 0]
    return [mask for mask in SECOND if mask in masks] + [mask for mask in masks if mask not in SECOND]


def score_kernel(n, me_ref, src_vmem, rows_ref, x_ref, head_ref, *refs):
    outs, (logits, src_ref, sem) = refs[: len(FIRST)], refs[len(FIRST) :]
    copy = pltpu.make_async_copy(src_vmem, src_ref, sem)
    copy.start()
    beams = x_ref.shape[0]
    blocks = head_ref.shape[1] // BLK
    group = 8 if blocks % 8 == 0 else 1
    for j in range(0, blocks, group):
        product = jnp.dot(x_ref[...], head_ref[:, j * BLK : (j + group) * BLK], preferred_element_type=jnp.float32)
        for i in range(group):
            logits[(j + i) * beams : (j + i + 1) * beams, :] = product[:, i * BLK : (i + 1) * BLK]
    most = functools.reduce(jnp.maximum, [logits[j * beams : (j + 1) * beams, :] for j in range(blocks)])
    most = jnp.max(most, axis=1, keepdims=True)
    total = sum(jnp.exp(logits[j * beams : (j + 1) * beams, :] - most) for j in range(blocks))
    lse = most + jnp.log(jnp.sum(total, axis=1, keepdims=True))
    hit = lax.broadcasted_iota(jnp.int32, (beams, rows_ref.shape[1]), 0) == rows_ref[...]
    ordered = jnp.sum(jnp.where(hit, lse, jnp.float32(0.0)), axis=0, keepdims=True)
    ordered = jnp.broadcast_to(ordered, (PAD, rows_ref.shape[1]))
    copy.wait()
    me = me_ref[0]
    second = second_masks(n)
    for i, a in enumerate(FIRST):
        for j, b in enumerate(second):
            owner = me ^ (a ^ b)
            for k in range(CAP):
                outs[i][j * CAP + k : j * CAP + k + 1, :] = logits[pl.ds(src_ref[k, owner], 1), :]
        for c in range(rows_ref.shape[1] // BLK):
            first = len(second) * CAP + c * PAD
            outs[i][first : first + PAD, :] = ordered[:, c * BLK : (c + 1) * BLK]


def place_kernel(n, rows_dev, slots, me_ref, place_ref, *refs):
    second = second_masks(n)
    own, others = refs[: len(FIRST)], refs[len(FIRST) : len(FIRST) + len(second) - 1]
    out_ref, held, stats = refs[-3:]
    wide = stats.shape[1] // BLK
    for i, a in enumerate(FIRST):
        for j, b in enumerate(second):
            d = a ^ b
            if j == 0:
                tiles, lse = own[i][:CAP, :], [own[i][len(second) * CAP + c * PAD : len(second) * CAP + c * PAD + 1, :] for c in range(wide)]
            else:
                tiles = others[j - 1][i * CAP : (i + 1) * CAP, :]
                lse = [others[j - 1][len(FIRST) * CAP + c * PAD + i : len(FIRST) * CAP + c * PAD + i + 1, :] for c in range(wide)]
            held[d * CAP : (d + 1) * CAP, :] = tiles
            for c in range(wide):
                stats[d : d + 1, c * BLK : (c + 1) * BLK] = lse[c]
    most = jnp.max(stats[...], axis=0, keepdims=True)
    lse = most + jnp.log(jnp.sum(jnp.exp(stats[...] - most), axis=0, keepdims=True))
    lane = lax.broadcasted_iota(jnp.int32, (rows_dev, stats.shape[1]), 1)
    row = lax.broadcasted_iota(jnp.int32, (rows_dev, stats.shape[1]), 0)
    lse = jnp.sum(jnp.where(lane == me_ref[0] * rows_dev + row, lse, jnp.float32(0.0)), axis=1, keepdims=True)
    left = held[...]
    place = place_ref[...].astype(jnp.bfloat16)
    tiles = jnp.zeros((rows_dev * slots, BLK), jnp.float32)
    for _ in range(3):
        part = left.astype(jnp.bfloat16)
        tiles += jnp.dot(place, part, preferred_element_type=jnp.float32)
        left -= part.astype(jnp.float32)
    valid = jnp.sum(place_ref[...], axis=1, keepdims=True) > 0
    for r in range(rows_dev):
        at = slice(r * slots, (r + 1) * slots)
        out_ref[r] = jnp.where(valid[at], tiles[at] - lse[r : r + 1, :], jnp.float32(0.0))


def in_vmem(x):
    return pltpu.with_memory_space_constraint(x, pltpu.VMEM)


def in_hbm(x):
    return pltpu.with_memory_space_constraint(x, pltpu.HBM)


def body(n, hidden, head, block_ids, valid_count, beam_order):
    me = lax.axis_index("vocab").astype(jnp.int32).reshape(1)
    rows_dev = hidden.shape[0]
    beams, slots = block_ids.shape
    blocks_dev = head.shape[1] // BLK
    fars = n // NEAR
    width = -(-beams // BLK) * BLK
    second = second_masks(n)
    anywhere = pl.BlockSpec(memory_space=pl.ANY)
    vmem = pl.BlockSpec(memory_space=pltpu.VMEM)
    smem = pl.BlockSpec(memory_space=pltpu.SMEM)
    hbm = pl.BlockSpec(memory_space=pltpu.HBM)

    far = [exchange(hidden, n, NEAR * f) for f in range(1, fars)]
    near = [exchange(hidden, n, mask) for mask in ORDER[1:]]
    far = far[0] if fars == 2 else jnp.concatenate(far, axis=0)
    mark = pl.pallas_call(
        mark_kernel,
        out_shape=jax.ShapeDtypeStruct((8, BLK), jnp.int32),
        in_specs=[smem],
        out_specs=vmem,
        cost_estimate=pl.CostEstimate(flops=2 * 10**10, bytes_accessed=0, transcendentals=0),
        compiler_params=pltpu.CompilerParams(vmem_limit_bytes=2**20),
        name="mark",
    )(me)

    src, row_of, place, kept = pl.pallas_call(
        functools.partial(index_kernel, n, rows_dev, blocks_dev),
        out_shape=[
            jax.ShapeDtypeStruct((CAP, n), jnp.int32),
            jax.ShapeDtypeStruct((1, width), jnp.int32),
            jax.ShapeDtypeStruct((rows_dev * slots, n * CAP), jnp.float32),
            pltpu.VMEM(hidden.shape, hidden.dtype),
        ],
        in_specs=[smem, hbm, hbm, hbm, anywhere, anywhere, hbm],
        out_specs=[vmem] * 4,
        scratch_shapes=[
            pltpu.VMEM((slots, beams), jnp.int32),
            pltpu.VMEM((1, beams), jnp.int32),
            pltpu.VMEM((1, beams), jnp.int32),
            pltpu.SemaphoreType.DMA((4,)),
        ],
        compiler_params=pltpu.CompilerParams(vmem_limit_bytes=4 * 2**20),
        name="index",
    )(
        me,
        in_hbm(block_ids.T),
        in_hbm(valid_count.reshape(1, beams)),
        in_hbm(beam_order.reshape(1, beams)),
        mark,
        far,
        in_hbm(hidden),
    )

    passed = [exchange(far, n, mask) for mask in ORDER[1:]]
    x = jnp.concatenate([far] + [part for pair in zip(near, passed) for part in pair] + [kept], axis=0)

    extra = width // BLK * PAD
    sent = pl.pallas_call(
        functools.partial(score_kernel, n),
        out_shape=[jax.ShapeDtypeStruct((len(second) * CAP + extra, BLK), jnp.float32)] * len(FIRST),
        in_specs=[smem, vmem, vmem, vmem, vmem],
        out_specs=[vmem] * len(FIRST),
        scratch_shapes=[
            pltpu.VMEM((blocks_dev * beams, BLK), jnp.float32),
            pltpu.SMEM((CAP, n), jnp.int32),
            pltpu.SemaphoreType.DMA,
        ],
        compiler_params=pltpu.CompilerParams(vmem_limit_bytes=24 * 2**20),
        name="score",
    )(me, in_vmem(src), in_vmem(row_of), in_vmem(x), in_vmem(head))

    own = [sent[0]] + [exchange(part, n, mask) for part, mask in zip(sent[1:], FIRST[1:])]
    at = lax.broadcasted_iota(jnp.int32, (extra, BLK), 0) % PAD
    stats = functools.reduce(
        lambda whole, i: jnp.where(at == i, own[i][len(second) * CAP :], whole), range(1, len(FIRST)), own[0][len(second) * CAP :]
    )
    others = [
        exchange(jnp.concatenate([part[j * CAP : (j + 1) * CAP] for part in own] + [stats]), n, mask)
        for j, mask in enumerate(second)
        if j
    ]
    return pl.pallas_call(
        functools.partial(place_kernel, n, rows_dev, slots),
        out_shape=jax.ShapeDtypeStruct((rows_dev, slots, BLK), jnp.float32),
        in_specs=[smem] + [vmem] * (1 + len(FIRST) + len(others)),
        out_specs=vmem,
        scratch_shapes=[pltpu.VMEM((n * CAP, BLK), jnp.float32), pltpu.VMEM((n, width), jnp.float32)],
        name="place",
    )(me, in_vmem(place), *map(in_vmem, own), *map(in_vmem, others))


def solution(mesh):
    return jax.shard_map(
        functools.partial(body, mesh.shape["vocab"]),
        mesh=mesh,
        in_specs=(P(("grp", "vocab"), None), P(None, "vocab"), P("grp", None), P("grp"), P("grp")),
        out_specs=P(("grp", "vocab"), None, None),
        check_vma=False,
    )
```

```python
import functools

import jax
import jax.numpy as jnp
from jax import lax
from jax.experimental import pallas as pl
from jax.experimental.pallas import tpu as pltpu
from jax.sharding import PartitionSpec as P

BLK = 128
CAP = 16
NEAR = 4
OWN = (3, 1, 2)
PASSED = (1, 3, 2)
FIRST = (0, 4)
SECOND = (0, 3, 1, 2)
GROUP = 2
ROWS = 128
PAD = 8


def exchange(x, n, mask):
    return lax.ppermute(x, "vocab", [(i, i ^ mask) for i in range(n)])


def split(n, rows_dev):
    beams = n * rows_dev
    at = lax.broadcasted_iota(jnp.int32, (beams, beams), 0)
    to = lax.broadcasted_iota(jnp.int32, (beams, beams), 1)
    shift = rows_dev.bit_length() - 1
    same = (at >> shift) == (to >> shift)
    return same.astype(jnp.bfloat16), (same & (at < to)).astype(jnp.bfloat16)


def mark_kernel(me_ref, out_ref):
    out_ref[...] = jnp.full(out_ref.shape, me_ref[0], jnp.int32)


def counts(a, b):
    return jnp.dot(a, b, preferred_element_type=jnp.float32)


def index_kernel(
    n,
    rows_dev,
    blocks_dev,
    me_ref,
    ids_hbm,
    valid_hbm,
    order_hbm,
    mark,
    after,
    hidden_hbm,
    src_ref,
    rows_ref,
    place_ref,
    own_ref,
    ids_ref,
    valid_ref,
    order_ref,
    sems,
):
    copies = [
        pltpu.make_async_copy(ids_hbm, ids_ref, sems.at[0]),
        pltpu.make_async_copy(valid_hbm, valid_ref, sems.at[1]),
        pltpu.make_async_copy(order_hbm, order_ref, sems.at[2]),
    ]
    own = pltpu.make_async_copy(hidden_hbm, own_ref, sems.at[3])
    for copy in copies + [own]:
        copy.start()
    for copy in copies:
        copy.wait()
    me = me_ref[0]
    slots, beams = ids_ref.shape
    shift = rows_dev.bit_length() - 1
    apart = (order_ref[...] >> shift) ^ me
    near = apart & (NEAR - 1)
    far = apart >> (NEAR.bit_length() - 1)
    fars = n // NEAR - 1
    row_of = jnp.where(far == 0, n - 1, far - 1)
    for i in range(NEAR - 1):
        row_of = jnp.where((near == OWN[i]) & (far == 0), fars + i, row_of)
        row_of = jnp.where((near == PASSED[i]) & (far > 0), fars * (i + 1) + NEAR - 2 + far, row_of)
    row_of = row_of * rows_dev
    row_of = row_of + (order_ref[...] & (rows_dev - 1))
    rows_ref[...] = jnp.full(rows_ref.shape, -1, jnp.int32)
    rows_ref[:, : order_ref.shape[1]] = row_of

    ids = ids_ref[...]
    same, earlier = split(n, rows_dev)
    k_at = lax.broadcasted_iota(jnp.int32, (slots, slots), 0)
    k_to = lax.broadcasted_iota(jnp.int32, (slots, slots), 1)
    below = (k_to < k_at).astype(jnp.bfloat16)

    def rank(on):
        ones = jnp.where(on, 1.0, 0.0).astype(jnp.bfloat16)
        return (counts(ones, earlier) + counts(below, counts(ones, same).astype(jnp.bfloat16))).astype(jnp.int32)

    at = jnp.zeros((slots, beams), jnp.int32)
    for d in range(n):
        on = (ids >= d * blocks_dev) & (ids < (d + 1) * blocks_dev)
        at = jnp.where(on, (me ^ d) * CAP + rank(on), at)
    k_index = lax.broadcasted_iota(jnp.int32, (slots, beams), 0)
    at = jnp.where(k_index < valid_ref[...], at, -1)
    row_index = lax.broadcasted_iota(jnp.int32, (slots, beams), 1)
    total = place_ref.shape[1]
    for r in range(rows_dev):
        column = jnp.sum(jnp.where(row_index == me * rows_dev + r, at, 0), axis=1, keepdims=True)
        hit = lax.broadcasted_iota(jnp.int32, (slots, total), 1) == column
        place_ref[r * slots : (r + 1) * slots, :] = jnp.where(hit, 1.0, 0.0)
    first = me * blocks_dev
    mine = (ids >= first) & (ids < first + blocks_dev)
    my_rank = jnp.where(mine, rank(mine), -1)
    local = ids - first
    owner = (
        (lax.broadcasted_iota(jnp.int32, (beams, n), 0) >> shift) == lax.broadcasted_iota(jnp.int32, (beams, n), 1)
    ).astype(jnp.bfloat16)
    rows = jnp.broadcast_to(row_of, (slots, beams))

    def gathered(value):
        picked = [jnp.sum(jnp.where(my_rank == j, value, 0), axis=0, keepdims=True) for j in range(CAP)]
        table = jnp.concatenate(picked, axis=0).astype(jnp.float32).astype(jnp.bfloat16)
        return counts(table, owner).astype(jnp.int32)

    src_ref[...] = gathered(local) * beams + gathered(rows)
    own.wait()


def second_masks(n):
    used = functools.reduce(lambda a, b: a | b, FIRST)
    masks = [mask for mask in range(n) if mask & used == 0]
    return [mask for mask in SECOND if mask in masks] + [mask for mask in masks if mask not in SECOND]


def score_kernel(n, me_ref, src_vmem, rows_ref, x_ref, head_ref, *refs):
    outs, (logits, src_ref, sem) = refs[: len(FIRST)], refs[len(FIRST) :]
    copy = pltpu.make_async_copy(src_vmem, src_ref, sem)
    copy.start()
    beams = x_ref.shape[0]
    blocks = head_ref.shape[1] // BLK
    group = GROUP if blocks % GROUP == 0 else 1
    wide = x_ref[...] if beams >= ROWS else jnp.concatenate([x_ref[...]] * (ROWS // beams))
    most = total = None
    for j in range(0, blocks, group):
        product = jnp.dot(wide, head_ref[:, j * BLK : (j + group) * BLK], preferred_element_type=jnp.float32)[:beams]
        tiles = [product[:, i * BLK : (i + 1) * BLK] for i in range(group)]
        for i, tile in enumerate(tiles):
            logits[(j + i) * beams : (j + i + 1) * beams, :] = tile
        higher = functools.reduce(jnp.maximum, tiles if most is None else [most] + tiles)
        terms = [jnp.exp(tile - higher) for tile in tiles]
        total = sum(terms if total is None else [total * jnp.exp(most - higher)] + terms)
        most = higher
    peak = jnp.max(most, axis=1, keepdims=True)
    lse = peak + jnp.log(jnp.sum(total * jnp.exp(most - peak), axis=1, keepdims=True))
    hit = lax.broadcasted_iota(jnp.int32, (beams, rows_ref.shape[1]), 0) == rows_ref[...]
    ordered = jnp.sum(jnp.where(hit, lse, jnp.float32(0.0)), axis=0, keepdims=True)
    ordered = jnp.broadcast_to(ordered, (PAD, rows_ref.shape[1]))
    copy.wait()
    me = me_ref[0]
    second = second_masks(n)
    for i, a in enumerate(FIRST):
        for j, b in enumerate(second):
            owner = me ^ (a ^ b)
            for k in range(CAP):
                outs[i][j * CAP + k : j * CAP + k + 1, :] = logits[pl.ds(src_ref[k, owner], 1), :]
        for c in range(rows_ref.shape[1] // BLK):
            first = len(second) * CAP + c * PAD
            outs[i][first : first + PAD, :] = ordered[:, c * BLK : (c + 1) * BLK]


def place_kernel(n, rows_dev, slots, me_ref, place_ref, *refs):
    second = second_masks(n)
    own, others = refs[: len(FIRST)], refs[len(FIRST) : len(FIRST) + len(second) - 1]
    out_ref, held, stats = refs[-3:]
    wide = stats.shape[1] // BLK
    for i, a in enumerate(FIRST):
        for j, b in enumerate(second):
            d = a ^ b
            if j == 0:
                tiles, lse = own[i][:CAP, :], [own[i][len(second) * CAP + c * PAD : len(second) * CAP + c * PAD + 1, :] for c in range(wide)]
            else:
                tiles = others[j - 1][i * CAP : (i + 1) * CAP, :]
                lse = [others[j - 1][len(FIRST) * CAP + c * PAD + i : len(FIRST) * CAP + c * PAD + i + 1, :] for c in range(wide)]
            held[d * CAP : (d + 1) * CAP, :] = tiles
            for c in range(wide):
                stats[d : d + 1, c * BLK : (c + 1) * BLK] = lse[c]
    most = jnp.max(stats[...], axis=0, keepdims=True)
    lse = most + jnp.log(jnp.sum(jnp.exp(stats[...] - most), axis=0, keepdims=True))
    lane = lax.broadcasted_iota(jnp.int32, (rows_dev, stats.shape[1]), 1)
    row = lax.broadcasted_iota(jnp.int32, (rows_dev, stats.shape[1]), 0)
    lse = jnp.sum(jnp.where(lane == me_ref[0] * rows_dev + row, lse, jnp.float32(0.0)), axis=1, keepdims=True)
    left = held[...]
    place = place_ref[...].astype(jnp.bfloat16)
    tiles = jnp.zeros((rows_dev * slots, BLK), jnp.float32)
    for _ in range(3):
        part = left.astype(jnp.bfloat16)
        tiles += jnp.dot(place, part, preferred_element_type=jnp.float32)
        left -= part.astype(jnp.float32)
    valid = jnp.sum(place_ref[...], axis=1, keepdims=True) > 0
    for r in range(rows_dev):
        at = slice(r * slots, (r + 1) * slots)
        out_ref[r] = jnp.where(valid[at], tiles[at] - lse[r : r + 1, :], jnp.float32(0.0))


def in_vmem(x):
    return pltpu.with_memory_space_constraint(x, pltpu.VMEM)


def in_hbm(x):
    return pltpu.with_memory_space_constraint(x, pltpu.HBM)


def body(n, hidden, head, block_ids, valid_count, beam_order):
    me = lax.axis_index("vocab").astype(jnp.int32).reshape(1)
    rows_dev = hidden.shape[0]
    beams, slots = block_ids.shape
    blocks_dev = head.shape[1] // BLK
    fars = n // NEAR
    width = -(-beams // BLK) * BLK
    second = second_masks(n)
    anywhere = pl.BlockSpec(memory_space=pl.ANY)
    vmem = pl.BlockSpec(memory_space=pltpu.VMEM)
    smem = pl.BlockSpec(memory_space=pltpu.SMEM)
    hbm = pl.BlockSpec(memory_space=pltpu.HBM)

    far = [exchange(hidden, n, NEAR * f) for f in range(1, fars)]
    near = [exchange(hidden, n, mask) for mask in OWN]
    far = far[0] if fars == 2 else jnp.concatenate(far, axis=0)
    mark = pl.pallas_call(
        mark_kernel,
        out_shape=jax.ShapeDtypeStruct((8, BLK), jnp.int32),
        in_specs=[smem],
        out_specs=vmem,
        cost_estimate=pl.CostEstimate(flops=2 * 10**10, bytes_accessed=0, transcendentals=0),
        compiler_params=pltpu.CompilerParams(vmem_limit_bytes=2**20),
        name="mark",
    )(me)

    src, row_of, place, kept = pl.pallas_call(
        functools.partial(index_kernel, n, rows_dev, blocks_dev),
        out_shape=[
            jax.ShapeDtypeStruct((CAP, n), jnp.int32),
            jax.ShapeDtypeStruct((1, width), jnp.int32),
            jax.ShapeDtypeStruct((rows_dev * slots, n * CAP), jnp.float32),
            pltpu.VMEM(hidden.shape, hidden.dtype),
        ],
        in_specs=[smem, hbm, hbm, hbm, anywhere, anywhere, hbm],
        out_specs=[vmem] * 4,
        scratch_shapes=[
            pltpu.VMEM((slots, beams), jnp.int32),
            pltpu.VMEM((1, beams), jnp.int32),
            pltpu.VMEM((1, beams), jnp.int32),
            pltpu.SemaphoreType.DMA((4,)),
        ],
        compiler_params=pltpu.CompilerParams(vmem_limit_bytes=4 * 2**20),
        name="index",
    )(
        me,
        in_hbm(block_ids.T),
        in_hbm(valid_count.reshape(1, beams)),
        in_hbm(beam_order.reshape(1, beams)),
        mark,
        far,
        in_hbm(hidden),
    )

    passed = [exchange(far, n, mask) for mask in PASSED]
    x = jnp.concatenate([far] + near + passed + [kept], axis=0)

    extra = width // BLK * PAD
    sent = pl.pallas_call(
        functools.partial(score_kernel, n),
        out_shape=[jax.ShapeDtypeStruct((len(second) * CAP + extra, BLK), jnp.float32)] * len(FIRST),
        in_specs=[smem, vmem, vmem, vmem, vmem],
        out_specs=[vmem] * len(FIRST),
        scratch_shapes=[
            pltpu.VMEM((blocks_dev * beams, BLK), jnp.float32),
            pltpu.SMEM((CAP, n), jnp.int32),
            pltpu.SemaphoreType.DMA,
        ],
        compiler_params=pltpu.CompilerParams(vmem_limit_bytes=24 * 2**20),
        name="score",
    )(me, in_vmem(src), in_vmem(row_of), in_vmem(x), in_vmem(head))

    own = [sent[0]] + [exchange(part, n, mask) for part, mask in zip(sent[1:], FIRST[1:])]
    at = lax.broadcasted_iota(jnp.int32, (extra, BLK), 0) % PAD
    stats = functools.reduce(
        lambda whole, i: jnp.where(at == i, own[i][len(second) * CAP :], whole), range(1, len(FIRST)), own[0][len(second) * CAP :]
    )
    others = [
        exchange(jnp.concatenate([part[j * CAP : (j + 1) * CAP] for part in own] + [stats]), n, mask)
        for j, mask in enumerate(second)
        if j
    ]
    return pl.pallas_call(
        functools.partial(place_kernel, n, rows_dev, slots),
        out_shape=jax.ShapeDtypeStruct((rows_dev, slots, BLK), jnp.float32),
        in_specs=[smem] + [vmem] * (1 + len(FIRST) + len(others)),
        out_specs=vmem,
        scratch_shapes=[pltpu.VMEM((n * CAP, BLK), jnp.float32), pltpu.VMEM((n, width), jnp.float32)],
        name="place",
    )(me, in_vmem(place), *map(in_vmem, own), *map(in_vmem, others))


def solution(mesh):
    return jax.shard_map(
        functools.partial(body, mesh.shape["vocab"]),
        mesh=mesh,
        in_specs=(P(("grp", "vocab"), None), P(None, "vocab"), P("grp", None), P("grp"), P("grp")),
        out_specs=P(("grp", "vocab"), None, None),
        check_vma=False,
    )
```

```python
import functools

import jax
import jax.numpy as jnp
from jax import lax
from jax.experimental import pallas as pl
from jax.experimental.pallas import tpu as pltpu
from jax.sharding import PartitionSpec as P

BLK = 128
CAP = 16
NEAR = 4
EARLY = (2, 1)
LATE = (3, 2, 1)
FIRST = (0, 4)
SECOND = (0, 3, 2, 1)
GROUP = 2
ROWS = 128
PAD = 8


def exchange(x, n, mask):
    return lax.ppermute(x, "vocab", [(i, i ^ mask) for i in range(n)])


def split(n, rows_dev):
    beams = n * rows_dev
    at = lax.broadcasted_iota(jnp.int32, (beams, beams), 0)
    to = lax.broadcasted_iota(jnp.int32, (beams, beams), 1)
    shift = rows_dev.bit_length() - 1
    same = (at >> shift) == (to >> shift)
    return same.astype(jnp.bfloat16), (same & (at < to)).astype(jnp.bfloat16)


def mark_kernel(me_ref, out_ref):
    out_ref[...] = jnp.full(out_ref.shape, me_ref[0], jnp.int32)


def counts(a, b):
    return jnp.dot(a, b, preferred_element_type=jnp.float32)


def layout(n):
    far = list(range(NEAR, n, NEAR))
    masks = list(EARLY)
    for near in LATE:
        masks += [near ^ mask for mask in ([] if near in EARLY else [0]) + far]
    return masks + [0] + far


def index_kernel(
    n,
    rows_dev,
    blocks_dev,
    me_ref,
    ids_hbm,
    valid_hbm,
    order_hbm,
    mark,
    after,
    src_ref,
    rows_ref,
    place_ref,
    ids_ref,
    valid_ref,
    order_ref,
    sems,
):
    copies = [
        pltpu.make_async_copy(ids_hbm, ids_ref, sems.at[0]),
        pltpu.make_async_copy(valid_hbm, valid_ref, sems.at[1]),
        pltpu.make_async_copy(order_hbm, order_ref, sems.at[2]),
    ]
    for copy in copies:
        copy.start()
    for copy in copies:
        copy.wait()
    me = me_ref[0]
    slots, beams = ids_ref.shape
    shift = rows_dev.bit_length() - 1
    apart = (order_ref[...] >> shift) ^ me
    row_of = sum(jnp.where(apart == mask, i * rows_dev, 0) for i, mask in enumerate(layout(n)))
    row_of = row_of + (order_ref[...] & (rows_dev - 1))
    rows_ref[...] = jnp.full(rows_ref.shape, -1, jnp.int32)
    rows_ref[:, : order_ref.shape[1]] = row_of

    ids = ids_ref[...]
    same, earlier = split(n, rows_dev)
    k_at = lax.broadcasted_iota(jnp.int32, (slots, slots), 0)
    k_to = lax.broadcasted_iota(jnp.int32, (slots, slots), 1)
    below = (k_to < k_at).astype(jnp.bfloat16)

    def rank(on):
        ones = jnp.where(on, 1.0, 0.0).astype(jnp.bfloat16)
        return (counts(ones, earlier) + counts(below, counts(ones, same).astype(jnp.bfloat16))).astype(jnp.int32)

    at = jnp.zeros((slots, beams), jnp.int32)
    for d in range(n):
        on = (ids >= d * blocks_dev) & (ids < (d + 1) * blocks_dev)
        at = jnp.where(on, (me ^ d) * CAP + rank(on), at)
    k_index = lax.broadcasted_iota(jnp.int32, (slots, beams), 0)
    at = jnp.where(k_index < valid_ref[...], at, -1)
    row_index = lax.broadcasted_iota(jnp.int32, (slots, beams), 1)
    total = place_ref.shape[1]
    for r in range(rows_dev):
        column = jnp.sum(jnp.where(row_index == me * rows_dev + r, at, 0), axis=1, keepdims=True)
        hit = lax.broadcasted_iota(jnp.int32, (slots, total), 1) == column
        place_ref[r * slots : (r + 1) * slots, :] = jnp.where(hit, 1.0, 0.0)
    first = me * blocks_dev
    mine = (ids >= first) & (ids < first + blocks_dev)
    my_rank = jnp.where(mine, rank(mine), -1)
    local = ids - first
    owner = (
        (lax.broadcasted_iota(jnp.int32, (beams, n), 0) >> shift) == lax.broadcasted_iota(jnp.int32, (beams, n), 1)
    ).astype(jnp.bfloat16)
    rows = jnp.broadcast_to(row_of, (slots, beams))

    def gathered(value):
        picked = [jnp.sum(jnp.where(my_rank == j, value, 0), axis=0, keepdims=True) for j in range(CAP)]
        table = jnp.concatenate(picked, axis=0).astype(jnp.float32).astype(jnp.bfloat16)
        return counts(table, owner).astype(jnp.int32)

    src_ref[...] = gathered(local) * beams + gathered(rows)


def second_masks(n):
    used = functools.reduce(lambda a, b: a | b, FIRST)
    masks = [mask for mask in range(n) if mask & used == 0]
    return [mask for mask in SECOND if mask in masks] + [mask for mask in masks if mask not in SECOND]


def score_kernel(n, me_ref, src_vmem, rows_ref, x_ref, head_ref, *refs):
    outs, (logits, src_ref, sem) = refs[: len(FIRST)], refs[len(FIRST) :]
    copy = pltpu.make_async_copy(src_vmem, src_ref, sem)
    copy.start()
    beams = x_ref.shape[0]
    blocks = head_ref.shape[1] // BLK
    group = GROUP if blocks % GROUP == 0 else 1
    wide = x_ref[...] if beams >= ROWS else jnp.concatenate([x_ref[...]] * (ROWS // beams))
    most = total = None
    for j in range(0, blocks, group):
        product = jnp.dot(wide, head_ref[:, j * BLK : (j + group) * BLK], preferred_element_type=jnp.float32)[:beams]
        tiles = [product[:, i * BLK : (i + 1) * BLK] for i in range(group)]
        for i, tile in enumerate(tiles):
            logits[(j + i) * beams : (j + i + 1) * beams, :] = tile
        higher = functools.reduce(jnp.maximum, tiles if most is None else [most] + tiles)
        terms = [jnp.exp(tile - higher) for tile in tiles]
        total = sum(terms if total is None else [total * jnp.exp(most - higher)] + terms)
        most = higher
    peak = jnp.max(most, axis=1, keepdims=True)
    lse = peak + jnp.log(jnp.sum(total * jnp.exp(most - peak), axis=1, keepdims=True))
    hit = lax.broadcasted_iota(jnp.int32, (beams, rows_ref.shape[1]), 0) == rows_ref[...]
    ordered = jnp.sum(jnp.where(hit, lse, jnp.float32(0.0)), axis=0, keepdims=True)
    ordered = jnp.broadcast_to(ordered, (PAD, rows_ref.shape[1]))
    copy.wait()
    me = me_ref[0]
    second = second_masks(n)
    for i, a in enumerate(FIRST):
        for j, b in enumerate(second):
            owner = me ^ (a ^ b)
            for k in range(CAP):
                outs[i][j * CAP + k : j * CAP + k + 1, :] = logits[pl.ds(src_ref[k, owner], 1), :]
        for c in range(rows_ref.shape[1] // BLK):
            first = len(second) * CAP + c * PAD
            outs[i][first : first + PAD, :] = ordered[:, c * BLK : (c + 1) * BLK]


def place_kernel(n, rows_dev, slots, me_ref, place_ref, *refs):
    second = second_masks(n)
    own, others = refs[: len(FIRST)], refs[len(FIRST) : len(FIRST) + len(second) - 1]
    out_ref, held, stats = refs[-3:]
    wide = stats.shape[1] // BLK
    for i, a in enumerate(FIRST):
        for j, b in enumerate(second):
            d = a ^ b
            if j == 0:
                tiles, lse = own[i][:CAP, :], [own[i][len(second) * CAP + c * PAD : len(second) * CAP + c * PAD + 1, :] for c in range(wide)]
            else:
                tiles = others[j - 1][i * CAP : (i + 1) * CAP, :]
                lse = [others[j - 1][len(FIRST) * CAP + c * PAD + i : len(FIRST) * CAP + c * PAD + i + 1, :] for c in range(wide)]
            held[d * CAP : (d + 1) * CAP, :] = tiles
            for c in range(wide):
                stats[d : d + 1, c * BLK : (c + 1) * BLK] = lse[c]
    most = jnp.max(stats[...], axis=0, keepdims=True)
    lse = most + jnp.log(jnp.sum(jnp.exp(stats[...] - most), axis=0, keepdims=True))
    lane = lax.broadcasted_iota(jnp.int32, (rows_dev, stats.shape[1]), 1)
    row = lax.broadcasted_iota(jnp.int32, (rows_dev, stats.shape[1]), 0)
    lse = jnp.sum(jnp.where(lane == me_ref[0] * rows_dev + row, lse, jnp.float32(0.0)), axis=1, keepdims=True)
    left = held[...]
    place = place_ref[...].astype(jnp.bfloat16)
    tiles = jnp.zeros((rows_dev * slots, BLK), jnp.float32)
    for _ in range(3):
        part = left.astype(jnp.bfloat16)
        tiles += jnp.dot(place, part, preferred_element_type=jnp.float32)
        left -= part.astype(jnp.float32)
    valid = jnp.sum(place_ref[...], axis=1, keepdims=True) > 0
    for r in range(rows_dev):
        at = slice(r * slots, (r + 1) * slots)
        out_ref[r] = jnp.where(valid[at], tiles[at] - lse[r : r + 1, :], jnp.float32(0.0))


def in_vmem(x):
    return pltpu.with_memory_space_constraint(x, pltpu.VMEM)


def in_hbm(x):
    return pltpu.with_memory_space_constraint(x, pltpu.HBM)


def body(n, hidden, head, block_ids, valid_count, beam_order):
    me = lax.axis_index("vocab").astype(jnp.int32).reshape(1)
    rows_dev = hidden.shape[0]
    beams, slots = block_ids.shape
    blocks_dev = head.shape[1] // BLK
    fars = n // NEAR
    width = -(-beams // BLK) * BLK
    second = second_masks(n)
    anywhere = pl.BlockSpec(memory_space=pl.ANY)
    vmem = pl.BlockSpec(memory_space=pltpu.VMEM)
    smem = pl.BlockSpec(memory_space=pltpu.SMEM)
    hbm = pl.BlockSpec(memory_space=pltpu.HBM)

    far = [exchange(hidden, n, NEAR * f) for f in range(1, fars)]
    near = [exchange(hidden, n, mask) for mask in EARLY]
    far = far[0] if fars == 2 else jnp.concatenate(far, axis=0)
    mark = pl.pallas_call(
        mark_kernel,
        out_shape=jax.ShapeDtypeStruct((8, BLK), jnp.int32),
        in_specs=[smem],
        out_specs=vmem,
        cost_estimate=pl.CostEstimate(flops=2 * 10**10, bytes_accessed=0, transcendentals=0),
        compiler_params=pltpu.CompilerParams(vmem_limit_bytes=2**20),
        name="mark",
    )(me)

    src, row_of, place = pl.pallas_call(
        functools.partial(index_kernel, n, rows_dev, blocks_dev),
        out_shape=[
            jax.ShapeDtypeStruct((CAP, n), jnp.int32),
            jax.ShapeDtypeStruct((1, width), jnp.int32),
            jax.ShapeDtypeStruct((rows_dev * slots, n * CAP), jnp.float32),
        ],
        in_specs=[smem, hbm, hbm, hbm, anywhere, anywhere],
        out_specs=[vmem] * 3,
        scratch_shapes=[
            pltpu.VMEM((slots, beams), jnp.int32),
            pltpu.VMEM((1, beams), jnp.int32),
            pltpu.VMEM((1, beams), jnp.int32),
            pltpu.SemaphoreType.DMA((3,)),
        ],
        compiler_params=pltpu.CompilerParams(vmem_limit_bytes=4 * 2**20),
        name="index",
    )(
        me,
        in_hbm(block_ids.T),
        in_hbm(valid_count.reshape(1, beams)),
        in_hbm(beam_order.reshape(1, beams)),
        mark,
        far,
    )

    both = jnp.concatenate([hidden, far], axis=0)
    late = [exchange(far if mask in EARLY else both, n, mask) for mask in LATE]
    x = jnp.concatenate([*near, *late, both], axis=0)

    extra = width // BLK * PAD
    sent = pl.pallas_call(
        functools.partial(score_kernel, n),
        out_shape=[jax.ShapeDtypeStruct((len(second) * CAP + extra, BLK), jnp.float32)] * len(FIRST),
        in_specs=[smem, vmem, vmem, vmem, vmem],
        out_specs=[vmem] * len(FIRST),
        scratch_shapes=[
            pltpu.VMEM((blocks_dev * beams, BLK), jnp.float32),
            pltpu.SMEM((CAP, n), jnp.int32),
            pltpu.SemaphoreType.DMA,
        ],
        compiler_params=pltpu.CompilerParams(vmem_limit_bytes=24 * 2**20),
        name="score",
    )(me, in_vmem(src), in_vmem(row_of), in_vmem(x), in_vmem(head))

    own = [sent[0]] + [exchange(part, n, mask) for part, mask in zip(sent[1:], FIRST[1:])]
    at = lax.broadcasted_iota(jnp.int32, (extra, BLK), 0) % PAD
    stats = functools.reduce(
        lambda whole, i: jnp.where(at == i, own[i][len(second) * CAP :], whole), range(1, len(FIRST)), own[0][len(second) * CAP :]
    )
    others = [
        exchange(jnp.concatenate([part[j * CAP : (j + 1) * CAP] for part in own] + [stats]), n, mask)
        for j, mask in enumerate(second)
        if j
    ]
    return pl.pallas_call(
        functools.partial(place_kernel, n, rows_dev, slots),
        out_shape=jax.ShapeDtypeStruct((rows_dev, slots, BLK), jnp.float32),
        in_specs=[smem] + [vmem] * (1 + len(FIRST) + len(others)),
        out_specs=vmem,
        scratch_shapes=[pltpu.VMEM((n * CAP, BLK), jnp.float32), pltpu.VMEM((n, width), jnp.float32)],
        name="place",
    )(me, in_vmem(place), *map(in_vmem, own), *map(in_vmem, others))


def solution(mesh):
    return jax.shard_map(
        functools.partial(body, mesh.shape["vocab"]),
        mesh=mesh,
        in_specs=(P(("grp", "vocab"), None), P(None, "vocab"), P("grp", None), P("grp"), P("grp")),
        out_specs=P(("grp", "vocab"), None, None),
        check_vma=False,
    )
```

```python
import functools

import jax
import jax.numpy as jnp
from jax import lax
from jax.experimental import pallas as pl
from jax.experimental.pallas import tpu as pltpu
from jax.sharding import PartitionSpec as P

BLK = 128
CAP = 16
NEAR = 4
EARLY = (2, 1)
LATE = (3, 2, 1)
FIRST = (0, 4)
SECOND = (0, 3, 2, 1)
GROUP = 2
ROWS = 128
PAD = 8


def exchange(x, n, mask):
    return lax.ppermute(x, "vocab", [(i, i ^ mask) for i in range(n)])


def split(n, rows_dev):
    beams = n * rows_dev
    at = lax.broadcasted_iota(jnp.int32, (beams, beams), 0)
    to = lax.broadcasted_iota(jnp.int32, (beams, beams), 1)
    shift = rows_dev.bit_length() - 1
    same = (at >> shift) == (to >> shift)
    return same.astype(jnp.bfloat16), (same & (at < to)).astype(jnp.bfloat16)


def mark_kernel(me_ref, out_ref):
    out_ref[...] = jnp.full(out_ref.shape, me_ref[0], jnp.int32)


def counts(a, b):
    return jnp.dot(a, b, preferred_element_type=jnp.float32)


def layout(n):
    far = list(range(NEAR, n, NEAR))
    masks = list(EARLY)
    for near in LATE:
        masks += [near ^ mask for mask in ([] if near in EARLY else [0]) + far]
    return masks + [0] + far


def index_kernel(
    n,
    rows_dev,
    blocks_dev,
    me_ref,
    ids_hbm,
    valid_hbm,
    order_hbm,
    mark,
    after,
    src_ref,
    rows_ref,
    place_ref,
    ids_ref,
    valid_ref,
    order_ref,
    sems,
):
    copies = [
        pltpu.make_async_copy(ids_hbm, ids_ref, sems.at[0]),
        pltpu.make_async_copy(valid_hbm, valid_ref, sems.at[1]),
        pltpu.make_async_copy(order_hbm, order_ref, sems.at[2]),
    ]
    for copy in copies:
        copy.start()
    for copy in copies:
        copy.wait()
    me = me_ref[0]
    slots, beams = ids_ref.shape
    shift = rows_dev.bit_length() - 1
    apart = (order_ref[...] >> shift) ^ me
    row_of = sum(jnp.where(apart == mask, i * rows_dev, 0) for i, mask in enumerate(layout(n)))
    row_of = row_of + (order_ref[...] & (rows_dev - 1))
    rows_ref[...] = jnp.full(rows_ref.shape, -1, jnp.int32)
    rows_ref[:, : order_ref.shape[1]] = row_of

    ids = ids_ref[...]
    same, earlier = split(n, rows_dev)
    k_at = lax.broadcasted_iota(jnp.int32, (slots, slots), 0)
    k_to = lax.broadcasted_iota(jnp.int32, (slots, slots), 1)
    below = (k_to < k_at).astype(jnp.bfloat16)

    def rank(on):
        ones = jnp.where(on, 1.0, 0.0).astype(jnp.bfloat16)
        return (counts(ones, earlier) + counts(below, counts(ones, same).astype(jnp.bfloat16))).astype(jnp.int32)

    at = jnp.zeros((slots, beams), jnp.int32)
    for d in range(n):
        on = (ids >= d * blocks_dev) & (ids < (d + 1) * blocks_dev)
        at = jnp.where(on, (me ^ d) * CAP + rank(on), at)
    k_index = lax.broadcasted_iota(jnp.int32, (slots, beams), 0)
    at = jnp.where(k_index < valid_ref[...], at, -1)
    row_index = lax.broadcasted_iota(jnp.int32, (slots, beams), 1)
    total = place_ref.shape[1]
    for r in range(rows_dev):
        column = jnp.sum(jnp.where(row_index == me * rows_dev + r, at, 0), axis=1, keepdims=True)
        hit = lax.broadcasted_iota(jnp.int32, (slots, total), 1) == column
        place_ref[r * slots : (r + 1) * slots, :] = jnp.where(hit, 1.0, 0.0)
    first = me * blocks_dev
    mine = (ids >= first) & (ids < first + blocks_dev)
    my_rank = jnp.where(mine, rank(mine), -1)
    local = ids - first
    owner = (
        (lax.broadcasted_iota(jnp.int32, (beams, n), 0) >> shift) == lax.broadcasted_iota(jnp.int32, (beams, n), 1)
    ).astype(jnp.bfloat16)
    rows = jnp.broadcast_to(row_of, (slots, beams))

    def gathered(value):
        picked = [jnp.sum(jnp.where(my_rank == j, value, 0), axis=0, keepdims=True) for j in range(CAP)]
        table = jnp.concatenate(picked, axis=0).astype(jnp.float32).astype(jnp.bfloat16)
        return counts(table, owner).astype(jnp.int32)

    src_ref[...] = gathered(local) * beams + gathered(rows)


def second_masks(n):
    used = functools.reduce(lambda a, b: a | b, FIRST)
    masks = [mask for mask in range(n) if mask & used == 0]
    return [mask for mask in SECOND if mask in masks] + [mask for mask in masks if mask not in SECOND]


def score_kernel(n, me_ref, src_vmem, rows_ref, x_ref, head_ref, *refs):
    outs, (logits, src_ref, sem) = refs[: len(FIRST)], refs[len(FIRST) :]
    copy = pltpu.make_async_copy(src_vmem, src_ref, sem)
    copy.start()
    beams = x_ref.shape[0]
    blocks = head_ref.shape[1] // BLK
    group = GROUP if blocks % GROUP == 0 else 1
    wide = x_ref[...] if beams >= ROWS else jnp.concatenate([x_ref[...]] * (ROWS // beams))
    most = total = None
    for j in range(0, blocks, group):
        product = jnp.dot(wide, head_ref[:, j * BLK : (j + group) * BLK], preferred_element_type=jnp.float32)[:beams]
        tiles = [product[:, i * BLK : (i + 1) * BLK] for i in range(group)]
        for i, tile in enumerate(tiles):
            logits[(j + i) * beams : (j + i + 1) * beams, :] = tile
        higher = functools.reduce(jnp.maximum, tiles if most is None else [most] + tiles)
        terms = [jnp.exp(tile - higher) for tile in tiles]
        total = sum(terms if total is None else [total * jnp.exp(most - higher)] + terms)
        most = higher
    peak = jnp.max(most, axis=1, keepdims=True)
    lse = peak + jnp.log(jnp.sum(total * jnp.exp(most - peak), axis=1, keepdims=True))
    hit = lax.broadcasted_iota(jnp.int32, (beams, rows_ref.shape[1]), 0) == rows_ref[...]
    ordered = jnp.sum(jnp.where(hit, lse, jnp.float32(0.0)), axis=0, keepdims=True)
    ordered = jnp.broadcast_to(ordered, (PAD, rows_ref.shape[1]))
    copy.wait()
    me = me_ref[0]
    second = second_masks(n)
    for i, a in enumerate(FIRST):
        for j, b in enumerate(second):
            owner = me ^ (a ^ b)
            for k in range(CAP):
                outs[i][j * CAP + k : j * CAP + k + 1, :] = logits[pl.ds(src_ref[k, owner], 1), :]
        for c in range(rows_ref.shape[1] // BLK):
            first = len(second) * CAP + c * PAD
            outs[i][first : first + PAD, :] = ordered[:, c * BLK : (c + 1) * BLK]


def place_kernel(n, rows_dev, slots, me_ref, place_ref, *refs):
    second = second_masks(n)
    own, others = refs[: len(FIRST)], refs[len(FIRST) : len(FIRST) + len(second) - 1]
    out_ref, held, stats = refs[-3:]
    wide = stats.shape[1] // BLK
    for i, a in enumerate(FIRST):
        for j, b in enumerate(second):
            d = a ^ b
            if j == 0:
                tiles, lse = own[i][:CAP, :], [own[i][len(second) * CAP + c * PAD : len(second) * CAP + c * PAD + 1, :] for c in range(wide)]
            else:
                tiles = others[j - 1][i * CAP : (i + 1) * CAP, :]
                lse = [others[j - 1][len(FIRST) * CAP + c * PAD + i : len(FIRST) * CAP + c * PAD + i + 1, :] for c in range(wide)]
            held[d * CAP : (d + 1) * CAP, :] = tiles
            for c in range(wide):
                stats[d : d + 1, c * BLK : (c + 1) * BLK] = lse[c]
    most = jnp.max(stats[...], axis=0, keepdims=True)
    lse = most + jnp.log(jnp.sum(jnp.exp(stats[...] - most), axis=0, keepdims=True))
    lane = lax.broadcasted_iota(jnp.int32, (rows_dev, stats.shape[1]), 1)
    row = lax.broadcasted_iota(jnp.int32, (rows_dev, stats.shape[1]), 0)
    lse = jnp.sum(jnp.where(lane == me_ref[0] * rows_dev + row, lse, jnp.float32(0.0)), axis=1, keepdims=True)
    left = held[...]
    place = place_ref[...].astype(jnp.bfloat16)
    tiles = jnp.zeros((rows_dev * slots, BLK), jnp.float32)
    most = float(jnp.finfo(jnp.bfloat16).max)
    for _ in range(3):
        part = jnp.clip(left, -most, most).astype(jnp.bfloat16)
        tiles += jnp.dot(place, part, preferred_element_type=jnp.float32)
        left -= part.astype(jnp.float32)
    valid = jnp.sum(place_ref[...], axis=1, keepdims=True) > 0
    for r in range(rows_dev):
        at = slice(r * slots, (r + 1) * slots)
        out_ref[r] = jnp.where(valid[at], tiles[at] - lse[r : r + 1, :], jnp.float32(0.0))


def in_vmem(x):
    return pltpu.with_memory_space_constraint(x, pltpu.VMEM)


def in_hbm(x):
    return pltpu.with_memory_space_constraint(x, pltpu.HBM)


def body(n, hidden, head, block_ids, valid_count, beam_order):
    me = lax.axis_index("vocab").astype(jnp.int32).reshape(1)
    rows_dev = hidden.shape[0]
    beams, slots = block_ids.shape
    blocks_dev = head.shape[1] // BLK
    fars = n // NEAR
    width = -(-beams // BLK) * BLK
    second = second_masks(n)
    anywhere = pl.BlockSpec(memory_space=pl.ANY)
    vmem = pl.BlockSpec(memory_space=pltpu.VMEM)
    smem = pl.BlockSpec(memory_space=pltpu.SMEM)
    hbm = pl.BlockSpec(memory_space=pltpu.HBM)

    far = [exchange(hidden, n, NEAR * f) for f in range(1, fars)]
    near = [exchange(hidden, n, mask) for mask in EARLY]
    far = far[0] if fars == 2 else jnp.concatenate(far, axis=0)
    mark = pl.pallas_call(
        mark_kernel,
        out_shape=jax.ShapeDtypeStruct((8, BLK), jnp.int32),
        in_specs=[smem],
        out_specs=vmem,
        cost_estimate=pl.CostEstimate(flops=2 * 10**10, bytes_accessed=0, transcendentals=0),
        compiler_params=pltpu.CompilerParams(vmem_limit_bytes=2**20),
        name="mark",
    )(me)

    src, row_of, place = pl.pallas_call(
        functools.partial(index_kernel, n, rows_dev, blocks_dev),
        out_shape=[
            jax.ShapeDtypeStruct((CAP, n), jnp.int32),
            jax.ShapeDtypeStruct((1, width), jnp.int32),
            jax.ShapeDtypeStruct((rows_dev * slots, n * CAP), jnp.float32),
        ],
        in_specs=[smem, hbm, hbm, hbm, anywhere, anywhere],
        out_specs=[vmem] * 3,
        scratch_shapes=[
            pltpu.VMEM((slots, beams), jnp.int32),
            pltpu.VMEM((1, beams), jnp.int32),
            pltpu.VMEM((1, beams), jnp.int32),
            pltpu.SemaphoreType.DMA((3,)),
        ],
        compiler_params=pltpu.CompilerParams(vmem_limit_bytes=4 * 2**20),
        name="index",
    )(
        me,
        in_hbm(block_ids.T),
        in_hbm(valid_count.reshape(1, beams)),
        in_hbm(beam_order.reshape(1, beams)),
        mark,
        far,
    )

    both = jnp.concatenate([hidden, far], axis=0)
    late = [exchange(far if mask in EARLY else both, n, mask) for mask in LATE]
    x = jnp.concatenate([*near, *late, both], axis=0)

    extra = width // BLK * PAD
    sent = pl.pallas_call(
        functools.partial(score_kernel, n),
        out_shape=[jax.ShapeDtypeStruct((len(second) * CAP + extra, BLK), jnp.float32)] * len(FIRST),
        in_specs=[smem, vmem, vmem, vmem, vmem],
        out_specs=[vmem] * len(FIRST),
        scratch_shapes=[
            pltpu.VMEM((blocks_dev * beams, BLK), jnp.float32),
            pltpu.SMEM((CAP, n), jnp.int32),
            pltpu.SemaphoreType.DMA,
        ],
        compiler_params=pltpu.CompilerParams(vmem_limit_bytes=24 * 2**20),
        name="score",
    )(me, in_vmem(src), in_vmem(row_of), in_vmem(x), in_vmem(head))

    own = [sent[0]] + [exchange(part, n, mask) for part, mask in zip(sent[1:], FIRST[1:])]
    at = lax.broadcasted_iota(jnp.int32, (extra, BLK), 0) % PAD
    stats = functools.reduce(
        lambda whole, i: jnp.where(at == i, own[i][len(second) * CAP :], whole), range(1, len(FIRST)), own[0][len(second) * CAP :]
    )
    others = [
        exchange(jnp.concatenate([part[j * CAP : (j + 1) * CAP] for part in own] + [stats]), n, mask)
        for j, mask in enumerate(second)
        if j
    ]
    return pl.pallas_call(
        functools.partial(place_kernel, n, rows_dev, slots),
        out_shape=jax.ShapeDtypeStruct((rows_dev, slots, BLK), jnp.float32),
        in_specs=[smem] + [vmem] * (1 + len(FIRST) + len(others)),
        out_specs=vmem,
        scratch_shapes=[pltpu.VMEM((n * CAP, BLK), jnp.float32), pltpu.VMEM((n, width), jnp.float32)],
        name="place",
    )(me, in_vmem(place), *map(in_vmem, own), *map(in_vmem, others))


def solution(mesh):
    return jax.shard_map(
        functools.partial(body, mesh.shape["vocab"]),
        mesh=mesh,
        in_specs=(P(("grp", "vocab"), None), P(None, "vocab"), P("grp", None), P("grp"), P("grp")),
        out_specs=P(("grp", "vocab"), None, None),
        check_vma=False,
    )
```

```python
import functools

import jax
import jax.numpy as jnp
from jax import lax
from jax.experimental import pallas as pl
from jax.experimental.pallas import tpu as pltpu
from jax.sharding import PartitionSpec as P

BLK = 128
CAP = 16
NEAR = 4
EARLY = (2, 1)
LATE = (3, 2, 1)
FIRST = (0, 3, 2, 1)
SECOND = (0, 4)
GROUP = 2
ROWS = 128
PAD = 8


def exchange(x, n, mask):
    return lax.ppermute(x, "vocab", [(i, i ^ mask) for i in range(n)])


def split(n, rows_dev):
    beams = n * rows_dev
    at = lax.broadcasted_iota(jnp.int32, (beams, beams), 0)
    to = lax.broadcasted_iota(jnp.int32, (beams, beams), 1)
    shift = rows_dev.bit_length() - 1
    same = (at >> shift) == (to >> shift)
    return same.astype(jnp.bfloat16), (same & (at < to)).astype(jnp.bfloat16)


def mark_kernel(me_ref, out_ref):
    out_ref[...] = jnp.full(out_ref.shape, me_ref[0], jnp.int32)


def counts(a, b):
    return jnp.dot(a, b, preferred_element_type=jnp.float32)


def layout(n):
    far = list(range(NEAR, n, NEAR))
    masks = list(EARLY)
    for near in LATE:
        masks += [near ^ mask for mask in ([] if near in EARLY else [0]) + far]
    return masks + [0] + far


def index_kernel(
    n,
    rows_dev,
    blocks_dev,
    me_ref,
    ids_hbm,
    valid_hbm,
    order_hbm,
    mark,
    after,
    src_ref,
    rows_ref,
    place_ref,
    ids_ref,
    valid_ref,
    order_ref,
    sems,
):
    copies = [
        pltpu.make_async_copy(ids_hbm, ids_ref, sems.at[0]),
        pltpu.make_async_copy(valid_hbm, valid_ref, sems.at[1]),
        pltpu.make_async_copy(order_hbm, order_ref, sems.at[2]),
    ]
    for copy in copies:
        copy.start()
    for copy in copies:
        copy.wait()
    me = me_ref[0]
    slots, beams = ids_ref.shape
    shift = rows_dev.bit_length() - 1
    apart = (order_ref[...] >> shift) ^ me
    row_of = sum(jnp.where(apart == mask, i * rows_dev, 0) for i, mask in enumerate(layout(n)))
    row_of = row_of + (order_ref[...] & (rows_dev - 1))
    rows_ref[...] = jnp.full(rows_ref.shape, -1, jnp.int32)
    rows_ref[:, : order_ref.shape[1]] = row_of

    ids = ids_ref[...]
    same, earlier = split(n, rows_dev)
    k_at = lax.broadcasted_iota(jnp.int32, (slots, slots), 0)
    k_to = lax.broadcasted_iota(jnp.int32, (slots, slots), 1)
    below = (k_to < k_at).astype(jnp.bfloat16)

    def rank(on):
        ones = jnp.where(on, 1.0, 0.0).astype(jnp.bfloat16)
        return (counts(ones, earlier) + counts(below, counts(ones, same).astype(jnp.bfloat16))).astype(jnp.int32)

    at = jnp.zeros((slots, beams), jnp.int32)
    for d in range(n):
        on = (ids >= d * blocks_dev) & (ids < (d + 1) * blocks_dev)
        at = jnp.where(on, (me ^ d) * CAP + rank(on), at)
    k_index = lax.broadcasted_iota(jnp.int32, (slots, beams), 0)
    at = jnp.where(k_index < valid_ref[...], at, -1)
    row_index = lax.broadcasted_iota(jnp.int32, (slots, beams), 1)
    total = place_ref.shape[1]
    for r in range(rows_dev):
        column = jnp.sum(jnp.where(row_index == me * rows_dev + r, at, 0), axis=1, keepdims=True)
        hit = lax.broadcasted_iota(jnp.int32, (slots, total), 1) == column
        place_ref[r * slots : (r + 1) * slots, :] = jnp.where(hit, 1.0, 0.0)
    first = me * blocks_dev
    mine = (ids >= first) & (ids < first + blocks_dev)
    my_rank = jnp.where(mine, rank(mine), -1)
    local = ids - first
    owner = (
        (lax.broadcasted_iota(jnp.int32, (beams, n), 0) >> shift) == lax.broadcasted_iota(jnp.int32, (beams, n), 1)
    ).astype(jnp.bfloat16)
    rows = jnp.broadcast_to(row_of, (slots, beams))

    def gathered(value):
        picked = [jnp.sum(jnp.where(my_rank == j, value, 0), axis=0, keepdims=True) for j in range(CAP)]
        table = jnp.concatenate(picked, axis=0).astype(jnp.float32).astype(jnp.bfloat16)
        return counts(table, owner).astype(jnp.int32)

    src_ref[...] = gathered(local) * beams + gathered(rows)


def second_masks(n):
    used = functools.reduce(lambda a, b: a | b, FIRST)
    masks = [mask for mask in range(n) if mask & used == 0]
    return [mask for mask in SECOND if mask in masks] + [mask for mask in masks if mask not in SECOND]


def score_kernel(n, me_ref, src_vmem, rows_ref, x_ref, head_ref, *refs):
    outs, (logits, src_ref, sem) = refs[: len(FIRST)], refs[len(FIRST) :]
    copy = pltpu.make_async_copy(src_vmem, src_ref, sem)
    copy.start()
    beams = x_ref.shape[0]
    blocks = head_ref.shape[1] // BLK
    group = GROUP if blocks % GROUP == 0 else 1
    wide = x_ref[...] if beams >= ROWS else jnp.concatenate([x_ref[...]] * (ROWS // beams))
    most = total = None
    for j in range(0, blocks, group):
        product = jnp.dot(wide, head_ref[:, j * BLK : (j + group) * BLK], preferred_element_type=jnp.float32)[:beams]
        tiles = [product[:, i * BLK : (i + 1) * BLK] for i in range(group)]
        for i, tile in enumerate(tiles):
            logits[(j + i) * beams : (j + i + 1) * beams, :] = tile
        higher = functools.reduce(jnp.maximum, tiles if most is None else [most] + tiles)
        terms = [jnp.exp(tile - higher) for tile in tiles]
        total = sum(terms if total is None else [total * jnp.exp(most - higher)] + terms)
        most = higher
    peak = jnp.max(most, axis=1, keepdims=True)
    lse = peak + jnp.log(jnp.sum(total * jnp.exp(most - peak), axis=1, keepdims=True))
    hit = lax.broadcasted_iota(jnp.int32, (beams, rows_ref.shape[1]), 0) == rows_ref[...]
    ordered = jnp.sum(jnp.where(hit, lse, jnp.float32(0.0)), axis=0, keepdims=True)
    ordered = jnp.broadcast_to(ordered, (PAD, rows_ref.shape[1]))
    copy.wait()
    me = me_ref[0]
    second = second_masks(n)
    for i, a in enumerate(FIRST):
        for j, b in enumerate(second):
            owner = me ^ (a ^ b)
            for k in range(CAP):
                outs[i][j * CAP + k : j * CAP + k + 1, :] = logits[pl.ds(src_ref[k, owner], 1), :]
        for c in range(rows_ref.shape[1] // BLK):
            first = len(second) * CAP + c * PAD
            outs[i][first : first + PAD, :] = ordered[:, c * BLK : (c + 1) * BLK]


def place_kernel(n, rows_dev, slots, me_ref, place_ref, *refs):
    second = second_masks(n)
    own, others = refs[: len(FIRST)], refs[len(FIRST) : len(FIRST) + len(second) - 1]
    out_ref, held, stats = refs[-3:]
    wide = stats.shape[1] // BLK
    for i, a in enumerate(FIRST):
        for j, b in enumerate(second):
            d = a ^ b
            if j == 0:
                tiles, lse = own[i][:CAP, :], [own[i][len(second) * CAP + c * PAD : len(second) * CAP + c * PAD + 1, :] for c in range(wide)]
            else:
                tiles = others[j - 1][i * CAP : (i + 1) * CAP, :]
                lse = [others[j - 1][len(FIRST) * CAP + c * PAD + i : len(FIRST) * CAP + c * PAD + i + 1, :] for c in range(wide)]
            held[d * CAP : (d + 1) * CAP, :] = tiles
            for c in range(wide):
                stats[d : d + 1, c * BLK : (c + 1) * BLK] = lse[c]
    most = jnp.max(stats[...], axis=0, keepdims=True)
    lse = most + jnp.log(jnp.sum(jnp.exp(stats[...] - most), axis=0, keepdims=True))
    lane = lax.broadcasted_iota(jnp.int32, (rows_dev, stats.shape[1]), 1)
    row = lax.broadcasted_iota(jnp.int32, (rows_dev, stats.shape[1]), 0)
    lse = jnp.sum(jnp.where(lane == me_ref[0] * rows_dev + row, lse, jnp.float32(0.0)), axis=1, keepdims=True)
    left = held[...]
    place = place_ref[...].astype(jnp.bfloat16)
    tiles = jnp.zeros((rows_dev * slots, BLK), jnp.float32)
    most = float(jnp.finfo(jnp.bfloat16).max)
    for _ in range(3):
        part = jnp.clip(left, -most, most).astype(jnp.bfloat16)
        tiles += jnp.dot(place, part, preferred_element_type=jnp.float32)
        left -= part.astype(jnp.float32)
    valid = jnp.sum(place_ref[...], axis=1, keepdims=True) > 0
    for r in range(rows_dev):
        at = slice(r * slots, (r + 1) * slots)
        out_ref[r] = jnp.where(valid[at], tiles[at] - lse[r : r + 1, :], jnp.float32(0.0))


def in_vmem(x):
    return pltpu.with_memory_space_constraint(x, pltpu.VMEM)


def in_hbm(x):
    return pltpu.with_memory_space_constraint(x, pltpu.HBM)


def body(n, hidden, head, block_ids, valid_count, beam_order):
    me = lax.axis_index("vocab").astype(jnp.int32).reshape(1)
    rows_dev = hidden.shape[0]
    beams, slots = block_ids.shape
    blocks_dev = head.shape[1] // BLK
    fars = n // NEAR
    width = -(-beams // BLK) * BLK
    second = second_masks(n)
    anywhere = pl.BlockSpec(memory_space=pl.ANY)
    vmem = pl.BlockSpec(memory_space=pltpu.VMEM)
    smem = pl.BlockSpec(memory_space=pltpu.SMEM)
    hbm = pl.BlockSpec(memory_space=pltpu.HBM)

    far = [exchange(hidden, n, NEAR * f) for f in range(1, fars)]
    near = [exchange(hidden, n, mask) for mask in EARLY]
    far = far[0] if fars == 2 else jnp.concatenate(far, axis=0)
    mark = pl.pallas_call(
        mark_kernel,
        out_shape=jax.ShapeDtypeStruct((8, BLK), jnp.int32),
        in_specs=[smem],
        out_specs=vmem,
        cost_estimate=pl.CostEstimate(flops=2 * 10**10, bytes_accessed=0, transcendentals=0),
        compiler_params=pltpu.CompilerParams(vmem_limit_bytes=2**20),
        name="mark",
    )(me)

    src, row_of, place = pl.pallas_call(
        functools.partial(index_kernel, n, rows_dev, blocks_dev),
        out_shape=[
            jax.ShapeDtypeStruct((CAP, n), jnp.int32),
            jax.ShapeDtypeStruct((1, width), jnp.int32),
            jax.ShapeDtypeStruct((rows_dev * slots, n * CAP), jnp.float32),
        ],
        in_specs=[smem, hbm, hbm, hbm, anywhere, anywhere],
        out_specs=[vmem] * 3,
        scratch_shapes=[
            pltpu.VMEM((slots, beams), jnp.int32),
            pltpu.VMEM((1, beams), jnp.int32),
            pltpu.VMEM((1, beams), jnp.int32),
            pltpu.SemaphoreType.DMA((3,)),
        ],
        compiler_params=pltpu.CompilerParams(vmem_limit_bytes=4 * 2**20),
        name="index",
    )(
        me,
        in_hbm(block_ids.T),
        in_hbm(valid_count.reshape(1, beams)),
        in_hbm(beam_order.reshape(1, beams)),
        mark,
        far,
    )

    both = jnp.concatenate([hidden, far], axis=0)
    late = [exchange(far if mask in EARLY else both, n, mask) for mask in LATE]
    x = jnp.concatenate([*near, *late, both], axis=0)

    extra = width // BLK * PAD
    sent = pl.pallas_call(
        functools.partial(score_kernel, n),
        out_shape=[jax.ShapeDtypeStruct((len(second) * CAP + extra, BLK), jnp.float32)] * len(FIRST),
        in_specs=[smem, vmem, vmem, vmem, vmem],
        out_specs=[vmem] * len(FIRST),
        scratch_shapes=[
            pltpu.VMEM((blocks_dev * beams, BLK), jnp.float32),
            pltpu.SMEM((CAP, n), jnp.int32),
            pltpu.SemaphoreType.DMA,
        ],
        compiler_params=pltpu.CompilerParams(vmem_limit_bytes=24 * 2**20),
        name="score",
    )(me, in_vmem(src), in_vmem(row_of), in_vmem(x), in_vmem(head))

    own = [sent[0]] + [exchange(part, n, mask) for part, mask in zip(sent[1:], FIRST[1:])]
    at = lax.broadcasted_iota(jnp.int32, (extra, BLK), 0) % PAD
    stats = functools.reduce(
        lambda whole, i: jnp.where(at == i, own[i][len(second) * CAP :], whole), range(1, len(FIRST)), own[0][len(second) * CAP :]
    )
    others = [
        exchange(jnp.concatenate([part[j * CAP : (j + 1) * CAP] for part in own] + [stats]), n, mask)
        for j, mask in enumerate(second)
        if j
    ]
    return pl.pallas_call(
        functools.partial(place_kernel, n, rows_dev, slots),
        out_shape=jax.ShapeDtypeStruct((rows_dev, slots, BLK), jnp.float32),
        in_specs=[smem] + [vmem] * (1 + len(FIRST) + len(others)),
        out_specs=vmem,
        scratch_shapes=[pltpu.VMEM((n * CAP, BLK), jnp.float32), pltpu.VMEM((n, width), jnp.float32)],
        name="place",
    )(me, in_vmem(place), *map(in_vmem, own), *map(in_vmem, others))


def solution(mesh):
    return jax.shard_map(
        functools.partial(body, mesh.shape["vocab"]),
        mesh=mesh,
        in_specs=(P(("grp", "vocab"), None), P(None, "vocab"), P("grp", None), P("grp"), P("grp")),
        out_specs=P(("grp", "vocab"), None, None),
        check_vma=False,
    )
```
